32 devices in a mesh: gx: 8 (over y, x, core), gz: 4 (over z).
Axes of the slice: x: 2, y: 2, z: 4, core: 2. Of those that a mesh axis runs over, the one named last changes fastest.
Arguments:
- elevation: float32 [2048, 2048], P(('gx', 'gz')), may hold values from -2 to 2
- potential: float32 [2048, 2048], P(('gx', 'gz')), may hold values from -6 to 6
- tracer: float32 [2048, 32, 256], P('gx', 'gz'), may hold values from -6 to 6
- wind_speed: float32 [2048, 32, 256], P('gx', 'gz'), may hold values from -4 to 4
Outputs:
- new_elevation: float32 [2048, 2048], P(('gx', 'gz'))
- new_tracer: float32 [2048, 32, 256], P('gx', 'gz')
The draws below stay inside these ranges and needn't reach their ends.
All inputs are finite; a program needn't handle non-finite values.
Results may differ from the reference program's by a relative error of at most 0.00019.
Values sent between devices are 32-bit elements; how exact they have to be, the bound alone decides.
A program may use at most 128 MiB of HBM per device.

```python
import jax
import jax.numpy as jnp

NS = 2048
YA = 256
LEV = 32


def steps_of(stream_key, extent, shards, smallest, largest):
    loudness = 1.0
    for axis_at, shards_of in shards:
        heights = jax.random.uniform(jax.random.fold_in(jax.random.fold_in(stream_key, 6), axis_at), (shards_of,), jnp.float32, smallest / len(shards), largest / len(shards))
        loudness = loudness * jnp.repeat(jnp.exp(heights), extent[axis_at] // shards_of).reshape((-1,) + (1,) * (len(extent) - 1 - axis_at))
    return loudness


def normal_values(key, extent, spread, reach, split=(), held_as=jnp.bfloat16):
    factor_of = steps_of(key, extent, split, -0.22, 0.18) if split else 1.0
    entries = jax.random.normal(key, extent, jnp.float32) * spread * factor_of
    return jnp.minimum(jnp.maximum(entries, -reach), reach).astype(held_as)


def setup_inputs(seed: int = 0) -> dict:
    keys = jax.random.split(jax.random.key(seed), 5)
    elevation = normal_values(keys[0], (NS, NS), 0.15, 2.0, ((0, 32),), jnp.float32)
    potential = normal_values(keys[1], (NS, NS), 1.0, 6.0, ((0, 32),), jnp.float32)
    tracer = normal_values(keys[2], (NS, LEV, YA), 1.0, 6.0, ((0, 8), (1, 4)), jnp.float32)
    wind_speed = normal_values(keys[3], (NS, LEV, YA), 1.0, 4.0, ((0, 8), (1, 4)), jnp.float32)
    return dict(elevation=elevation, potential=potential, tracer=tracer, wind_speed=wind_speed)


TWO_PI = 6.283185307179586
DT_WAVE = 0.05
COLUMN_DEPTH = 32.0
DT_AIR = 0.1
NU_AIR = 0.2

def wave_numbers(length):
    positions = jnp.arange(length, dtype=jnp.int32)
    signed = jnp.where(positions < length // 2, positions, positions - length).astype(jnp.float32) * (TWO_PI / length)
    odd_wave = jnp.where(positions == length // 2, 0.0, signed)
    return (signed, odd_wave)

def to_field(spectrum):
    return jnp.real(jnp.fft.ifft2(spectrum)).astype(jnp.float32)

def mirror_levels(field):
    lower_level = jnp.concatenate([field[:, :1], field[:, :-1]], 1)
    upper_level = jnp.concatenate([field[:, 1:], field[:, -1:]], 1)
    return (lower_level, upper_level)

def reference(elevation, potential, tracer, wind_speed):
    signed, odd_wave = wave_numbers(NS)
    magnitude = jnp.sqrt(signed[:, None] * signed[:, None] + signed[None, :] * signed[None, :])
    squared = magnitude * magnitude
    magnitude_cube = squared * magnitude
    along_x = 1j * odd_wave[:, None]
    along_y = 1j * odd_wave[None, :]
    eta_spec = jnp.fft.fft2(elevation)
    phi_spec = jnp.fft.fft2(potential)
    first_once = to_field(magnitude * phi_spec)
    first_twice = to_field(squared * phi_spec)
    first_thrice = to_field(magnitude_cube * phi_spec)
    slope_x = to_field(along_x * eta_spec)
    slope_y = to_field(along_y * eta_spec)
    speed_x = to_field(along_x * phi_spec)
    speed_y = to_field(along_y * phi_spec)
    second_field = -elevation * first_once
    second_spec = jnp.fft.fft2(second_field)
    second_once = to_field(magnitude * second_spec)
    second_twice = to_field(squared * second_spec)
    third_field = -elevation * second_once - 0.5 * elevation * elevation * first_twice
    third_once = to_field(magnitude * jnp.fft.fft2(third_field))
    vertical = first_once + elevation * first_twice + 0.5 * elevation * elevation * first_thrice + second_once + elevation * second_twice + third_once
    tendency = -(slope_x * speed_x + slope_y * speed_y) + (1.0 + slope_x * slope_x + slope_y * slope_y) * vertical
    new_elevation = elevation + DT_WAVE * tendency
    new_slope = to_field(along_x * jnp.fft.fft2(new_elevation))
    old_rows = elevation[:, :YA]
    new_rows = new_elevation[:, :YA]
    slope_rows = new_slope[:, :YA]
    eastern = jnp.roll(tracer, -1, 0)
    western = jnp.roll(tracer, 1, 0)
    northern = jnp.concatenate([tracer[:, :, 1:], tracer[:, :, -1:]], 2)
    southern = jnp.concatenate([tracer[:, :, :1], tracer[:, :, :-1]], 2)
    moved_tracer = tracer + DT_AIR * (-wind_speed * (eastern - western) * 0.5 + NU_AIR * (eastern + western + northern + southern - 4.0 * tracer))
    sigma_level = (jnp.arange(LEV, dtype=jnp.int32).astype(jnp.float32) + 0.5) / LEV
    lift_factor = (1.0 - sigma_level)[None, :, None]
    level_shift = ((new_rows - old_rows) / (COLUMN_DEPTH - old_rows))[:, None, :] * lift_factor * LEV
    lower_level, upper_level = mirror_levels(moved_tracer)
    remapped = moved_tracer + 0.5 * level_shift * (upper_level - lower_level) + 0.5 * level_shift * level_shift * (upper_level - 2.0 * moved_tracer + lower_level)
    lower_level, upper_level = mirror_levels(remapped)
    column_depth = (COLUMN_DEPTH - new_rows)[:, None, :]
    advection = wind_speed * lift_factor * slope_rows[:, None, :] / column_depth * (upper_level - lower_level) * (0.5 * LEV)
    spread_term = NU_AIR * (upper_level - 2.0 * remapped + lower_level) * (LEV * LEV) / (column_depth * column_depth)
    new_tracer = remapped + DT_AIR * (advection + spread_term)
    return (new_elevation, new_tracer)
```

```python
import functools

import jax
import jax.numpy as jnp
import numpy as np
import ml_dtypes
from jax import lax
from jax.experimental import pallas as pl
from jax.experimental.pallas import tpu as pltpu
from jax.sharding import PartitionSpec as P

DT_WAVE = 0.05
COLUMN_DEPTH = 32.0
DT_AIR = 0.1
NU_AIR = 0.2
INNER = 128
VMEM_LIMIT = 60 * 1024 * 1024


def split_hi_lo(matrix):
    matrix = matrix.astype(np.float32)
    hi = matrix.astype(ml_dtypes.bfloat16)
    lo = (matrix - hi.astype(np.float32)).astype(ml_dtypes.bfloat16)
    return np.stack([hi, lo])


def slot_waves(length):
    outer = length // INNER
    half = INNER // 2
    lane = np.arange(INNER)
    first = np.where(lane < half, outer * lane, outer // 2 + outer * (lane - half))
    rest = [j + outer * lane for j in range(1, outer // 2)]
    return np.stack([first] + rest)


def signed_wave(k, length):
    k = k % length
    return np.where(k < length // 2, k, k - length) * (2 * np.pi / length)


@functools.lru_cache(None)
def row_tables(length):
    outer = length // INNER
    groups = outer // 2
    half = INNER // 2
    b = np.arange(INNER)
    waves = slot_waves(length)
    forward = np.zeros((groups, 2 * INNER, 2 * INNER))
    inverse = np.zeros((groups, 2 * INNER, 2 * INNER))
    for j in range(groups):
        theta = 2 * np.pi * ((b[:, None] * waves[j][None, :]) % length) / length
        c, s = np.cos(theta), np.sin(theta)
        if j:
            forward[j] = np.block([[c, -s], [s, c]])
            inverse[j] = 2.0 * np.block([[c.T, s.T], [-s.T, c.T]]) / length
            continue
        for part, cols in ((0, slice(0, half)), (1, slice(half, INNER))):
            rows = slice(part * INNER, (part + 1) * INNER)
            imag = slice(INNER + cols.start, INNER + cols.stop)
            forward[j][rows, cols] = c[:, cols]
            forward[j][rows, imag] = -s[:, cols]
            inverse[j][cols, rows] = 2.0 * c[:, cols].T / length
            inverse[j][imag, rows] = -2.0 * s[:, cols].T / length
        alternating = np.where(b % 2 == 0, 1.0, -1.0)
        forward[j][:INNER, INNER] = alternating
        inverse[j][0, :INNER] = 1.0 / length
        inverse[j][INNER, :INNER] = alternating / length
    odd = signed_wave(waves, length)
    odd[0, 0] = 0.0
    odd = np.concatenate([-odd, odd], 1).astype(np.float32)
    return split_hi_lo(forward), split_hi_lo(inverse), odd


@functools.lru_cache(None)
def column_tables(length, parts):
    rows = length // parts
    i = np.arange(rows)
    theta = 2 * np.pi * ((i[:, None] * i[None, :]) % rows) / rows
    c, s = np.cos(theta), np.sin(theta)
    forward = np.block([[c, -s], [s, c]])
    inverse = np.block([[c, s], [-s, c]]) / length
    k1 = np.arange(parts)
    twist = 2 * np.pi * ((k1[:, None] * i[None, :]) % length) / length
    cosine = np.concatenate([np.cos(twist)] * 2, 1)
    sine = np.concatenate([np.sin(twist), -np.sin(twist)], 1)
    k = k1[:, None] + parts * i[None, :]
    wave = signed_wave(k, length)
    odd = np.where(k == length // 2, 0.0, wave)
    wave = np.concatenate([wave, wave], 1)
    odd = np.concatenate([-odd, odd], 1)
    small = np.stack([cosine, sine, wave, odd]).astype(np.float32)
    return np.stack([split_hi_lo(forward), split_hi_lo(inverse)]), small


def dot3(x, hi_matrix, lo_matrix):
    hi = x.astype(jnp.bfloat16)
    lo = (x - hi.astype(jnp.float32)).astype(jnp.bfloat16)
    out = jnp.dot(hi, hi_matrix, preferred_element_type=jnp.float32)
    out += jnp.dot(lo, hi_matrix, preferred_element_type=jnp.float32)
    return out + jnp.dot(hi, lo_matrix, preferred_element_type=jnp.float32)


def constant_product(value, factor):
    if abs(factor) < 1e-12:
        return None
    if abs(factor - 1) < 1e-12:
        return value
    if abs(factor + 1) < 1e-12:
        return -value
    return value * np.float32(factor)


def total(terms):
    terms = [t for t in terms if t is not None]
    result = terms[0]
    for t in terms[1:]:
        result = result + t
    return result


def row_forward(field, table):
    outer = field.shape[1] // INNER
    half = outer // 2
    x = [field[:, a * INNER : (a + 1) * INNER] for a in range(outer)]
    plus = [x[a] + x[outer - a] for a in range(1, half)]
    minus = [x[a] - x[outer - a] for a in range(1, half)]
    ends = [x[0] + x[half], x[0] - x[half]]
    quarter = half // 2

    def real_of(k):
        sign = 1 if k % 2 == 0 else -1
        folded = []
        for a in range(1, quarter):
            both = plus[a - 1] + plus[half - a - 1] if sign > 0 else plus[a - 1] - plus[half - a - 1]
            folded.append(constant_product(both, np.cos(2 * np.pi * a * k / outer)))
        folded.append(constant_product(plus[quarter - 1], np.cos(2 * np.pi * quarter * k / outer)))
        return total([ends[k % 2]] + folded)

    def imag_of(k):
        folded = []
        for a in range(1, quarter):
            both = minus[a - 1] - minus[half - a - 1] if k % 2 == 0 else minus[a - 1] + minus[half - a - 1]
            folded.append(constant_product(both, -np.sin(2 * np.pi * a * k / outer)))
        folded.append(constant_product(minus[quarter - 1], -np.sin(2 * np.pi * quarter * k / outer)))
        return total(folded)

    groups = []
    for j in range(half):
        if j == 0:
            pair = jnp.concatenate([real_of(0), real_of(half)], 1)
        else:
            pair = jnp.concatenate([real_of(j), imag_of(j)], 1)
        groups.append(dot3(pair, table[0, j], table[1, j]))
    return groups


def row_inverse(groups, table):
    half = len(groups)
    outer = 2 * half
    y = [dot3(groups[j], table[0, j], table[1, j]) for j in range(half)]
    re = [v[:, :INNER] for v in y]
    im = [v[:, INNER:] for v in y]
    ends = [re[0] + im[0], re[0] - im[0]]
    blocks = [None] * outer
    for a in range(half + 1):
        even = total(
            [ends[a % 2]]
            + [constant_product(re[k], np.cos(2 * np.pi * a * k / outer)) for k in range(1, half)]
        )
        if a % half == 0:
            blocks[a] = even
            continue
        odd = total([constant_product(im[k], np.sin(2 * np.pi * a * k / outer)) for k in range(1, half)])
        blocks[a] = even - odd
        blocks[outer - a] = even + odd
    return jnp.concatenate(blocks, 1)


def put_groups(groups, out_ref):
    for j, g in enumerate(groups):
        both = jnp.concatenate([g[:, :INNER], g[:, INNER:]], 0)
        out_ref[j * INNER : (j + 1) * INNER, :] = both.T


def get_groups(in_ref):
    groups = []
    for j in range(in_ref.shape[0] // INNER):
        both = in_ref[j * INNER : (j + 1) * INNER, :].T
        rows = both.shape[0] // 2
        groups.append(jnp.concatenate([both[:rows], both[rows:]], 1))
    return groups


def y_derivative(groups, odd_ref, table):
    turned = []
    for j, g in enumerate(groups):
        turned.append(jnp.concatenate([g[:, INNER:], g[:, :INNER]], 1) * odd_ref[j : j + 1, :])
    return row_inverse(turned, table)


def turn(z):
    rows = z.shape[-1] // 2
    if z.shape[-1] == INNER:
        return pltpu.roll(z, rows, z.ndim - 1)
    return jnp.concatenate([z[..., rows:], z[..., :rows]], -1)


def list_transform(z, sign, signs):
    n = len(z)
    if n == 1:
        return z
    even = list_transform(z[0::2], sign, signs)
    odd = list_transform(z[1::2], sign, signs)
    first, second = [], []
    for k in range(n // 2):
        t = odd[k]
        if k:
            angle = sign * 2 * np.pi * k / n
            t = total(
                [
                    constant_product(t, np.cos(angle)),
                    turn(t) * (signs * np.float32(np.sin(angle))),
                ]
            )
        first.append(even[k] + t)
        second.append(even[k] - t)
    return first + second


def lane_signs(shape):
    lane = lax.broadcasted_iota(jnp.int32, shape, 1)
    return jnp.where(lane < shape[1] // 2, -1.0, 1.0).astype(jnp.float32)


def column_forward(z, matrix, small):
    y = list_transform(z, -1, lane_signs(z[0].shape))
    depth = z[0].shape[0]
    y = [v * small[0, k : k + 1] + turn(v) * small[1, k : k + 1] for k, v in enumerate(y)]
    out = dot3(jnp.concatenate(y, 0), matrix[0, 0], matrix[0, 1])
    return [out[k * depth : (k + 1) * depth] for k in range(len(z))]


def column_inverse(spectrum, matrix, small):
    depth = spectrum[0].shape[0]
    out = dot3(jnp.concatenate(spectrum, 0), matrix[1, 0], matrix[1, 1])
    y = [out[k * depth : (k + 1) * depth] for k in range(len(spectrum))]
    y = [v * small[0, k : k + 1] - turn(v) * small[1, k : k + 1] for k, v in enumerate(y)]
    return list_transform(y, 1, lane_signs(y[0].shape))


def open_columns(in_ref, first_mask, second_mask):
    z = []
    for s in range(in_ref.shape[0]):
        block = in_ref[s]
        head = block[:8]
        extra = turn(head) * first_mask
        head = head * (1.0 - second_mask)
        body = [block[8:]] if block.shape[0] > 8 else []
        z.append(jnp.concatenate([head] + body + [extra], 0))
    return z


def close_columns(z, out_ref, second_mask):
    for s, block in enumerate(z):
        depth = block.shape[0] - 8
        head = block[:8] * (1.0 - second_mask) + turn(block[depth:]) * second_mask
        out_ref[s, :8] = head
        if depth > 8:
            out_ref[s, 8:] = block[8:depth]


def masks(flag_ref):
    flag = flag_ref[...]
    row = lax.broadcasted_iota(jnp.int32, flag.shape, 0)
    lane = lax.broadcasted_iota(jnp.int32, flag.shape, 1)
    left = lane < flag.shape[1] // 2
    return (
        jnp.where((row == 0) & left, flag, 0.0),
        jnp.where((row == 0) & jnp.logical_not(left), flag, 0.0),
    )


def columns_kernel(powers, derivative, in_ref, flag_ref, wave_ref, matrix, small, *out_refs):
    first_mask, second_mask = masks(flag_ref)
    spectrum = column_forward(open_columns(in_ref, first_mask, second_mask), matrix, small)
    wave_y = wave_ref[...]
    y_squared = wave_y * wave_y
    squares = [small[2, k : k + 1] * small[2, k : k + 1] + y_squared for k in range(len(spectrum))]
    place = 0
    for power in powers:
        work = []
        for k, v in enumerate(spectrum):
            if power == 1:
                factor = jnp.sqrt(squares[k])
            elif power == 2:
                factor = squares[k]
            else:
                factor = squares[k] * jnp.sqrt(squares[k])
            work.append(v * factor)
        close_columns(column_inverse(work, matrix, small), out_refs[place], second_mask)
        place += 1
    if derivative:
        work = [turn(v) * small[3, k : k + 1] for k, v in enumerate(spectrum)]
        close_columns(column_inverse(work, matrix, small), out_refs[place], second_mask)


def slope_kernel(in_ref, matrix, small, out_ref):
    rows = in_ref.shape[2]
    z = []
    for s in range(in_ref.shape[0]):
        block = in_ref[s]
        z.append(jnp.concatenate([block, jnp.zeros_like(block)], 1))
    spectrum = column_forward(z, matrix, small)
    work = [turn(v) * small[3, k : k + 1] for k, v in enumerate(spectrum)]
    for s, block in enumerate(column_inverse(work, matrix, small)):
        out_ref[s] = block[:, :rows]


def first_kernel(p_ref, forward, out_ref):
    put_groups(row_forward(p_ref[...], forward), out_ref)


def side_kernel(e_ref, p_ref, forward, inverse, odd, out_ref, slope_ref, speed_ref):
    groups = row_forward(e_ref[...], forward)
    put_groups(groups, out_ref)
    slope_ref[...] = y_derivative(groups, odd, inverse)
    groups = row_forward(p_ref[...], forward)
    speed_ref[...] = y_derivative(groups, odd, inverse)


def second_kernel(e_ref, a0_ref, forward, inverse, first_once_ref, out_ref):
    first_once = row_inverse(get_groups(a0_ref), inverse)
    first_once_ref[...] = first_once
    put_groups(row_forward(-e_ref[...] * first_once, forward), out_ref)


def third_kernel(e_ref, b0_ref, a1_ref, forward, inverse, once_ref, twice_ref, out_ref):
    elevation = e_ref[...]
    once = row_inverse(get_groups(b0_ref), inverse)
    once_ref[...] = once
    twice = row_inverse(get_groups(a1_ref), inverse)
    twice_ref[...] = twice
    put_groups(
        row_forward(-elevation * once - 0.5 * elevation * elevation * twice, forward), out_ref
    )


def late_kernel(
    e_ref, a2_ref, b1_ref, sx_ref, vx_ref, sy_ref, vy_ref, first_ref, once_ref, twice_ref,
    inverse, part_ref, metric_ref, grad_ref,
):
    elevation = e_ref[...]
    thrice = row_inverse(get_groups(a2_ref), inverse)
    second_twice = row_inverse(get_groups(b1_ref), inverse)
    slope_x = row_inverse(get_groups(sx_ref), inverse)
    speed_x = row_inverse(get_groups(vx_ref), inverse)
    slope_y = sy_ref[...]
    part_ref[...] = (
        first_ref[...]
        + elevation * twice_ref[...]
        + 0.5 * elevation * elevation * thrice
        + once_ref[...]
        + elevation * second_twice
    )
    metric_ref[...] = 1.0 + slope_x * slope_x + slope_y * slope_y
    grad_ref[...] = slope_x * speed_x + slope_y * vy_ref[...]


def last_kernel(e_ref, c0_ref, part_ref, metric_ref, grad_ref, inverse, out_ref):
    vertical = part_ref[...] + row_inverse(get_groups(c0_ref), inverse)
    out_ref[...] = e_ref[...] + DT_WAVE * (metric_ref[...] * vertical - grad_ref[...])


def call(kernel, out_shapes, *args):
    single = not isinstance(out_shapes, list)
    shapes = [out_shapes] if single else out_shapes
    spec = pl.BlockSpec(memory_space=pltpu.VMEM)
    result = pl.pallas_call(
        kernel,
        out_shape=[jax.ShapeDtypeStruct(s, jnp.float32) for s in shapes],
        in_specs=[spec] * len(args),
        out_specs=[spec] * len(shapes),
        compiler_params=pltpu.CompilerParams(vmem_limit_bytes=VMEM_LIMIT),
    )(*args)
    return result[0] if single else result


def exchange(x):
    return lax.all_to_all(x, ("gx", "gz"), split_axis=0, concat_axis=0, tiled=True)


def neighbours(field, axis, dim, width, wrap):
    size, length = lax.axis_size(axis), field.shape[dim]
    up = [(i, (i + 1) % size) for i in range(size if wrap else size - 1)]
    down = [(j, i) for i, j in up]
    before = lax.ppermute(lax.slice_in_dim(field, length - width, length, axis=dim), axis, up)
    after = lax.ppermute(lax.slice_in_dim(field, 0, width, axis=dim), axis, down)
    return before, after


def remap(m, lower, upper, shift):
    return m + 0.5 * shift * (upper - lower) + 0.5 * shift * shift * (upper - 2.0 * m + lower)


def shards(elevation, potential, tracer, wind_speed):
    rows, length = elevation.shape
    gz = lax.axis_size("gz")
    gx = lax.axis_size("gx")
    parts = gx * gz
    depth = (length // 2) // parts
    wide = 2 * rows
    forward, inverse, odd = [jnp.asarray(t) for t in row_tables(length)]
    matrix, small = [jnp.asarray(t) for t in column_tables(length, parts)]
    device = lax.axis_index("gx") * gz + lax.axis_index("gz")
    waves = jnp.asarray(signed_wave(slot_waves(length), length).reshape(-1).astype(np.float32))
    mine = lax.dynamic_slice_in_dim(waves, device * depth, depth)
    mine = jnp.concatenate([mine, jnp.full((8,), np.float32(-np.pi))])
    wave_y = jnp.broadcast_to(mine[:, None], (depth + 8, wide))
    flag = jnp.broadcast_to((device == 0).astype(jnp.float32), (8, wide))
    half = (length // 2, wide)
    cols = (parts, depth, wide)
    field = (rows, length)

    def columns(x, powers, derivative):
        outs = [cols] * (len(powers) + (1 if derivative else 0))
        kernel = functools.partial(columns_kernel, powers, derivative)
        return call(kernel, outs, x, flag, wave_y, matrix, small)

    def send_columns(x):
        return exchange(x.reshape(cols))

    def send_rows(x):
        return exchange(x).reshape(half)

    p_half = call(first_kernel, half, potential, forward)
    p_cols = send_columns(p_half)
    e_half, slope_y, speed_y = call(
        side_kernel, [half, field, field], elevation, potential, forward, inverse, odd
    )
    e_cols = send_columns(e_half)
    a0, a1, a2, vx = columns(p_cols, (1, 2, 3), True)
    a0 = send_rows(a0)
    a1 = send_rows(a1)
    first_once, s_half = call(second_kernel, [field, half], elevation, a0, forward, inverse)
    s_cols = send_columns(s_half)
    (sx,) = columns(e_cols, (), True)
    a2 = send_rows(a2)
    b0, b1 = columns(s_cols, (1, 2), False)
    b0 = send_rows(b0)
    second_once, first_twice, t_half = call(
        third_kernel, [field, field, half], elevation, b0, a1, forward, inverse
    )
    t_cols = send_columns(t_half)
    vx = send_rows(vx)
    sx = send_rows(sx)
    b1 = send_rows(b1)
    (c0,) = columns(t_cols, (1,), False)
    c0 = send_rows(c0)
    part, metric, grad = call(
        late_kernel, [field, field, field], elevation, a2, b1, sx, vx, slope_y, speed_y,
        first_once, second_once, first_twice, inverse,
    )
    new_elevation = call(last_kernel, field, elevation, c0, part, metric, grad, inverse)

    air = tracer.shape[2]
    west, east = neighbours(tracer, "gx", 0, 1, True)
    eastern = jnp.concatenate([tracer[1:], east], 0)
    western = jnp.concatenate([west, tracer[:-1]], 0)
    northern = jnp.concatenate([tracer[:, :, 1:], tracer[:, :, -1:]], 2)
    southern = jnp.concatenate([tracer[:, :, :1], tracer[:, :, :-1]], 2)
    moved = tracer + DT_AIR * (
        -wind_speed * (eastern - western) * 0.5
        + NU_AIR * (eastern + western + northern + southern - 4.0 * tracer)
    )
    below, above = neighbours(moved, "gz", 1, 2, False)
    bottom = lax.axis_index("gz") == 0
    top = lax.axis_index("gz") == gz - 1
    below_near = jnp.where(bottom, moved[:, :1], below[:, 1:])
    above_near = jnp.where(top, moved[:, -1:], above[:, :1])

    window = new_elevation[:, :air]
    share = air // parts
    turned = window.reshape(rows, parts, share).transpose(1, 2, 0)
    turned = exchange(turned)
    slopes = call(slope_kernel, (parts, share, rows), turned, matrix, small)
    slopes = slopes.reshape(gx, 1, gz, share, rows)
    slopes = jnp.broadcast_to(slopes, (gx, gz, gz, share, rows)).reshape(parts, gz, share, rows)
    slopes = exchange(slopes)
    slope_rows = slopes.transpose(1, 3, 0, 2).reshape(gz * rows, air)
    old_rows = lax.all_gather(elevation[:, :air], "gz", axis=0, tiled=True)
    new_rows = lax.all_gather(window, "gz", axis=0, tiled=True)

    levels = tracer.shape[1]
    level_count = levels * gz
    base = lax.axis_index("gz") * levels
    level = (base - 1 + jnp.arange(levels + 2, dtype=jnp.int32)).astype(jnp.float32)
    lift = (1.0 - (level + 0.5) / level_count)[None, :, None]
    rise = ((new_rows - old_rows) / (COLUMN_DEPTH - old_rows))[:, None, :]
    shift = rise * lift[:, 1:-1] * level_count
    lower = jnp.concatenate([below_near, moved[:, :-1]], 1)
    upper = jnp.concatenate([moved[:, 1:], above_near], 1)
    remapped = remap(moved, lower, upper, shift)
    r_below = remap(below[:, 1:], below[:, :1], moved[:, :1], rise * lift[:, :1] * level_count)
    r_above = remap(above[:, :1], moved[:, -1:], above[:, 1:], rise * lift[:, -1:] * level_count)
    r_below = jnp.where(bottom, remapped[:, :1], r_below)
    r_above = jnp.where(top, remapped[:, -1:], r_above)
    lower = jnp.concatenate([r_below, remapped[:, :-1]], 1)
    upper = jnp.concatenate([remapped[:, 1:], r_above], 1)
    column = (COLUMN_DEPTH - new_rows)[:, None, :]
    advection = (
        wind_speed * lift[:, 1:-1] * slope_rows[:, None, :] / column
        * (upper - lower) * (0.5 * level_count)
    )
    spread = (
        NU_AIR * (upper - 2.0 * remapped + lower) * (level_count * level_count) / (column * column)
    )
    new_tracer = remapped + DT_AIR * (advection + spread)
    return (new_elevation, new_tracer)


def solution(mesh):
    return jax.shard_map(
        shards,
        mesh=mesh,
        in_specs=(
            P(("gx", "gz"), None),
            P(("gx", "gz"), None),
            P("gx", "gz", None),
            P("gx", "gz", None),
        ),
        out_specs=(P(("gx", "gz"), None), P("gx", "gz", None)),
        check_vma=False,
    )
```

```python
import functools

import jax
import jax.numpy as jnp
import numpy as np
import ml_dtypes
from jax import lax
from jax.experimental import pallas as pl
from jax.experimental.pallas import tpu as pltpu
from jax.sharding import PartitionSpec as P

DT_WAVE = 0.05
COLUMN_DEPTH = 32.0
DT_AIR = 0.1
NU_AIR = 0.2
INNER = 128
VMEM_LIMIT = 60 * 1024 * 1024


def split_hi_lo(matrix):
    matrix = matrix.astype(np.float32)
    hi = matrix.astype(ml_dtypes.bfloat16)
    lo = (matrix - hi.astype(np.float32)).astype(ml_dtypes.bfloat16)
    return np.stack([hi, lo])


def slot_waves(length):
    outer = length // INNER
    half = INNER // 2
    lane = np.arange(INNER)
    first = np.where(lane < half, outer * lane, outer // 2 + outer * (lane - half))
    rest = [j + outer * lane for j in range(1, outer // 2)]
    return np.stack([first] + rest)


def signed_wave(k, length):
    k = k % length
    return np.where(k < length // 2, k, k - length) * (2 * np.pi / length)


@functools.lru_cache(None)
def row_tables(length):
    outer = length // INNER
    groups = outer // 2
    half = INNER // 2
    b = np.arange(INNER)
    waves = slot_waves(length)
    forward = np.zeros((groups, 2 * INNER, 2 * INNER))
    inverse = np.zeros((groups, 2 * INNER, 2 * INNER))
    for j in range(groups):
        theta = 2 * np.pi * ((b[:, None] * waves[j][None, :]) % length) / length
        c, s = np.cos(theta), np.sin(theta)
        if j:
            forward[j] = np.block([[c, -s], [s, c]])
            inverse[j] = 2.0 * np.block([[c.T, s.T], [-s.T, c.T]]) / length
            continue
        for part, cols in ((0, slice(0, half)), (1, slice(half, INNER))):
            rows = slice(part * INNER, (part + 1) * INNER)
            imag = slice(INNER + cols.start, INNER + cols.stop)
            forward[j][rows, cols] = c[:, cols]
            forward[j][rows, imag] = -s[:, cols]
            inverse[j][cols, rows] = 2.0 * c[:, cols].T / length
            inverse[j][imag, rows] = -2.0 * s[:, cols].T / length
        alternating = np.where(b % 2 == 0, 1.0, -1.0)
        forward[j][:INNER, INNER] = alternating
        inverse[j][0, :INNER] = 1.0 / length
        inverse[j][INNER, :INNER] = alternating / length
    odd = signed_wave(waves, length)
    odd[0, 0] = 0.0
    odd = np.concatenate([-odd, odd], 1).astype(np.float32)
    return split_hi_lo(forward), split_hi_lo(inverse), odd


@functools.lru_cache(None)
def column_tables(length, parts):
    rows = length // parts
    i = np.arange(rows)
    theta = 2 * np.pi * ((i[:, None] * i[None, :]) % rows) / rows
    c, s = np.cos(theta), np.sin(theta)
    forward = np.block([[c, -s], [s, c]])
    inverse = np.block([[c, s], [-s, c]]) / length
    k1 = np.arange(parts)
    twist = 2 * np.pi * ((k1[:, None] * i[None, :]) % length) / length
    cosine = np.concatenate([np.cos(twist)] * 2, 1)
    sine = np.concatenate([np.sin(twist), -np.sin(twist)], 1)
    k = k1[:, None] + parts * i[None, :]
    wave = signed_wave(k, length)
    odd = np.where(k == length // 2, 0.0, wave)
    wave = np.concatenate([wave, wave], 1)
    odd = np.concatenate([-odd, odd], 1)
    small = np.stack([cosine, sine, wave, odd]).astype(np.float32)
    return np.stack([split_hi_lo(forward), split_hi_lo(inverse)]), small


def dot3(x, hi_matrix, lo_matrix):
    hi = x.astype(jnp.bfloat16)
    lo = (x - hi.astype(jnp.float32)).astype(jnp.bfloat16)
    out = jnp.dot(hi, hi_matrix, preferred_element_type=jnp.float32)
    out += jnp.dot(lo, hi_matrix, preferred_element_type=jnp.float32)
    return out + jnp.dot(hi, lo_matrix, preferred_element_type=jnp.float32)


def constant_product(value, factor):
    if abs(factor) < 1e-12:
        return None
    if abs(factor - 1) < 1e-12:
        return value
    if abs(factor + 1) < 1e-12:
        return -value
    return value * np.float32(factor)


def total(terms):
    terms = [t for t in terms if t is not None]
    result = terms[0]
    for t in terms[1:]:
        result = result + t
    return result


def row_forward(field, table):
    outer = field.shape[1] // INNER
    half = outer // 2
    x = [field[:, a * INNER : (a + 1) * INNER] for a in range(outer)]
    plus = [x[a] + x[outer - a] for a in range(1, half)]
    minus = [x[a] - x[outer - a] for a in range(1, half)]
    ends = [x[0] + x[half], x[0] - x[half]]
    quarter = half // 2

    def real_of(k):
        sign = 1 if k % 2 == 0 else -1
        folded = []
        for a in range(1, quarter):
            both = plus[a - 1] + plus[half - a - 1] if sign > 0 else plus[a - 1] - plus[half - a - 1]
            folded.append(constant_product(both, np.cos(2 * np.pi * a * k / outer)))
        folded.append(constant_product(plus[quarter - 1], np.cos(2 * np.pi * quarter * k / outer)))
        return total([ends[k % 2]] + folded)

    def imag_of(k):
        folded = []
        for a in range(1, quarter):
            both = minus[a - 1] - minus[half - a - 1] if k % 2 == 0 else minus[a - 1] + minus[half - a - 1]
            folded.append(constant_product(both, -np.sin(2 * np.pi * a * k / outer)))
        folded.append(constant_product(minus[quarter - 1], -np.sin(2 * np.pi * quarter * k / outer)))
        return total(folded)

    groups = []
    for j in range(half):
        if j == 0:
            pair = jnp.concatenate([real_of(0), real_of(half)], 1)
        else:
            pair = jnp.concatenate([real_of(j), imag_of(j)], 1)
        groups.append(dot3(pair, table[0, j], table[1, j]))
    return groups


def row_inverse(groups, table):
    half = len(groups)
    outer = 2 * half
    y = [dot3(groups[j], table[0, j], table[1, j]) for j in range(half)]
    re = [v[:, :INNER] for v in y]
    im = [v[:, INNER:] for v in y]
    ends = [re[0] + im[0], re[0] - im[0]]
    blocks = [None] * outer
    for a in range(half + 1):
        even = total(
            [ends[a % 2]]
            + [constant_product(re[k], np.cos(2 * np.pi * a * k / outer)) for k in range(1, half)]
        )
        if a % half == 0:
            blocks[a] = even
            continue
        odd = total([constant_product(im[k], np.sin(2 * np.pi * a * k / outer)) for k in range(1, half)])
        blocks[a] = even - odd
        blocks[outer - a] = even + odd
    return jnp.concatenate(blocks, 1)


def put_groups(groups, out_ref):
    for j, g in enumerate(groups):
        both = jnp.concatenate([g[:, :INNER], g[:, INNER:]], 0)
        out_ref[j * INNER : (j + 1) * INNER, :] = both.T


def get_groups(in_ref):
    groups = []
    for j in range(in_ref.shape[0] // INNER):
        both = in_ref[j * INNER : (j + 1) * INNER, :].T
        rows = both.shape[0] // 2
        groups.append(jnp.concatenate([both[:rows], both[rows:]], 1))
    return groups


def y_derivative(groups, odd_ref, table):
    turned = []
    for j, g in enumerate(groups):
        turned.append(jnp.concatenate([g[:, INNER:], g[:, :INNER]], 1) * odd_ref[j : j + 1, :])
    return row_inverse(turned, table)


def turn(z):
    rows = z.shape[-1] // 2
    if z.shape[-1] == INNER:
        return pltpu.roll(z, rows, z.ndim - 1)
    return jnp.concatenate([z[..., rows:], z[..., :rows]], -1)


def list_transform(z, sign, signs):
    n = len(z)
    if n == 1:
        return z
    even = list_transform(z[0::2], sign, signs)
    odd = list_transform(z[1::2], sign, signs)
    first, second = [], []
    for k in range(n // 2):
        t = odd[k]
        if k:
            angle = sign * 2 * np.pi * k / n
            t = total(
                [
                    constant_product(t, np.cos(angle)),
                    turn(t) * (signs * np.float32(np.sin(angle))),
                ]
            )
        first.append(even[k] + t)
        second.append(even[k] - t)
    return first + second


def lane_signs(shape):
    lane = lax.broadcasted_iota(jnp.int32, shape, 1)
    return jnp.where(lane < shape[1] // 2, -1.0, 1.0).astype(jnp.float32)


def column_forward(z, matrix, small):
    y = list_transform(z, -1, lane_signs(z[0].shape))
    depth = z[0].shape[0]
    y = [v * small[0, k : k + 1] + turn(v) * small[1, k : k + 1] for k, v in enumerate(y)]
    out = dot3(jnp.concatenate(y, 0), matrix[0, 0], matrix[0, 1])
    return [out[k * depth : (k + 1) * depth] for k in range(len(z))]


def column_inverse(spectrum, matrix, small):
    depth = spectrum[0].shape[0]
    out = dot3(jnp.concatenate(spectrum, 0), matrix[1, 0], matrix[1, 1])
    y = [out[k * depth : (k + 1) * depth] for k in range(len(spectrum))]
    y = [v * small[0, k : k + 1] - turn(v) * small[1, k : k + 1] for k, v in enumerate(y)]
    return list_transform(y, 1, lane_signs(y[0].shape))


def open_columns(in_ref, parts, first_mask, second_mask):
    z = []
    depth = in_ref.shape[0] // parts
    for s in range(parts):
        head = in_ref[s * depth : s * depth + 8]
        extra = turn(head) * first_mask
        head = head * (1.0 - second_mask)
        body = [in_ref[s * depth + 8 : (s + 1) * depth]] if depth > 8 else []
        z.append(jnp.concatenate([head] + body + [extra], 0))
    return z


def close_columns(z, out_ref, second_mask):
    for s, block in enumerate(z):
        depth = block.shape[0] - 8
        head = block[:8] * (1.0 - second_mask) + turn(block[depth:]) * second_mask
        out_ref[s * depth : s * depth + 8] = head
        if depth > 8:
            out_ref[s * depth + 8 : (s + 1) * depth] = block[8:depth]


def masks(flag_ref):
    flag = flag_ref[...]
    row = lax.broadcasted_iota(jnp.int32, flag.shape, 0)
    lane = lax.broadcasted_iota(jnp.int32, flag.shape, 1)
    left = lane < flag.shape[1] // 2
    return (
        jnp.where((row == 0) & left, flag, 0.0),
        jnp.where((row == 0) & jnp.logical_not(left), flag, 0.0),
    )


def slope_kernel(in_ref, matrix, small, out_ref):
    rows = in_ref.shape[2]
    z = []
    for s in range(in_ref.shape[0]):
        block = in_ref[s]
        z.append(jnp.concatenate([block, jnp.zeros_like(block)], 1))
    spectrum = column_forward(z, matrix, small)
    work = [turn(v) * small[3, k : k + 1] for k, v in enumerate(spectrum)]
    for s, block in enumerate(column_inverse(work, matrix, small)):
        out_ref[s] = block[:, :rows]


def surface_kernel(
    gx, gz, e_ref, p_ref, flag_ref, wave_ref, forward, inverse, odd, matrix, small,
    out_ref, *scratch,
):
    parts = gx * gz
    count = 12
    sent = scratch[:count]
    came = scratch[count : 2 * count]
    slope_y_ref, speed_y_ref, first_ref, twice_ref, part_ref, send_sem, recv_sem = scratch[2 * count :]
    depth = sent[0].shape[0] // parts
    at_x, at_z = lax.axis_index("gx"), lax.axis_index("gz")
    me = at_x * gz + at_z
    barrier = pltpu.get_barrier_semaphore()

    def peer_of(step):
        peer = lax.rem(me + step, parts)
        return peer, (peer // gz, lax.rem(peer, gz))

    def greet(step, carry):
        _, place = peer_of(step)
        pl.semaphore_signal(barrier, inc=1, device_id=place, device_id_type=pl.DeviceIdType.MESH)
        return carry

    def rows_at(index):
        return pl.ds(pl.multiple_of(index * depth, depth), depth)

    def send(k):
        def body(step, carry):
            peer, place = peer_of(step)
            pltpu.make_async_remote_copy(
                src_ref=sent[k].at[rows_at(peer)],
                dst_ref=came[k].at[rows_at(me)],
                send_sem=send_sem.at[k],
                recv_sem=recv_sem.at[k],
                device_id=place,
                device_id_type=pl.DeviceIdType.MESH,
            ).start()
            return carry

        lax.fori_loop(1, parts, body, 0)
        came[k][rows_at(me), :] = sent[k][rows_at(me), :]

    def whole(k):
        most = pl.ds(0, (parts - 1) * depth)
        return pltpu.make_async_remote_copy(
            src_ref=sent[k].at[most],
            dst_ref=came[k].at[most],
            send_sem=send_sem.at[k],
            recv_sem=recv_sem.at[k],
            device_id=peer_of(1)[1],
            device_id_type=pl.DeviceIdType.MESH,
        )

    def fetch(k):
        whole(k).wait_recv()

    first_mask, second_mask = masks(flag_ref)
    wave_y = wave_ref[...]
    y_squared = wave_y * wave_y

    def spectrum_of(k):
        return column_forward(open_columns(came[k], parts, first_mask, second_mask), matrix, small)

    def raised(spectrum, power, k):
        work = []
        for j, v in enumerate(spectrum):
            square = small[2, j : j + 1] * small[2, j : j + 1] + y_squared
            if power == 1:
                factor = jnp.sqrt(square)
            elif power == 2:
                factor = square
            else:
                factor = square * jnp.sqrt(square)
            work.append(v * factor)
        close_columns(column_inverse(work, matrix, small), sent[k], second_mask)

    def along_x(spectrum, k):
        work = [turn(v) * small[3, j : j + 1] for j, v in enumerate(spectrum)]
        close_columns(column_inverse(work, matrix, small), sent[k], second_mask)

    def field_of(k):
        return row_inverse(get_groups(came[k]), inverse)

    P0, E0, A0, A1, A2, VX, SX, S0, B0, B1, T0, C0 = range(count)
    lax.fori_loop(1, parts, greet, 0)
    p_groups = row_forward(p_ref[...], forward)
    put_groups(p_groups, sent[P0])
    pl.semaphore_wait(barrier, parts - 1)
    send(P0)
    e_groups = row_forward(e_ref[...], forward)
    put_groups(e_groups, sent[E0])
    send(E0)
    slope_y_ref[...] = y_derivative(e_groups, odd, inverse)
    speed_y_ref[...] = y_derivative(p_groups, odd, inverse)

    fetch(P0)
    p_spectrum = spectrum_of(P0)
    raised(p_spectrum, 1, A0)
    send(A0)
    raised(p_spectrum, 2, A1)
    send(A1)
    raised(p_spectrum, 3, A2)
    along_x(p_spectrum, VX)
    fetch(E0)
    along_x(spectrum_of(E0), SX)

    fetch(A0)
    first_ref[...] = field_of(A0)
    put_groups(row_forward(-e_ref[...] * first_ref[...], forward), sent[S0])
    send(S0)
    send(A2)
    fetch(A1)
    twice_ref[...] = field_of(A1)
    elevation = e_ref[...]
    part_ref[...] = first_ref[...] + elevation * twice_ref[...]

    fetch(S0)
    s_spectrum = spectrum_of(S0)
    raised(s_spectrum, 1, B0)
    send(B0)
    send(VX)
    raised(s_spectrum, 2, B1)
    fetch(A2)
    elevation = e_ref[...]
    part_ref[...] += 0.5 * elevation * elevation * field_of(A2)

    fetch(B0)
    once = field_of(B0)
    elevation = e_ref[...]
    third = -elevation * once - 0.5 * elevation * elevation * twice_ref[...]
    put_groups(row_forward(third, forward), sent[T0])
    send(T0)
    send(SX)
    send(B1)
    part_ref[...] += once
    fetch(VX)
    first_ref[...] = field_of(VX)

    fetch(T0)
    raised(spectrum_of(T0), 1, C0)
    send(C0)
    fetch(SX)
    slope_x = field_of(SX)
    slope_y = slope_y_ref[...]
    twice_ref[...] = 1.0 + slope_x * slope_x + slope_y * slope_y
    first_ref[...] = slope_x * first_ref[...] + slope_y * speed_y_ref[...]
    fetch(B1)
    part_ref[...] += e_ref[...] * field_of(B1)
    fetch(C0)
    vertical = part_ref[...] + field_of(C0)
    out_ref[...] = e_ref[...] + DT_WAVE * (twice_ref[...] * vertical - first_ref[...])
    for k in range(count):
        whole(k).wait_send()


def call(kernel, out_shapes, *args):
    single = not isinstance(out_shapes, list)
    shapes = [out_shapes] if single else out_shapes
    spec = pl.BlockSpec(memory_space=pltpu.VMEM)
    result = pl.pallas_call(
        kernel,
        out_shape=[jax.ShapeDtypeStruct(s, jnp.float32) for s in shapes],
        in_specs=[spec] * len(args),
        out_specs=[spec] * len(shapes),
        compiler_params=pltpu.CompilerParams(vmem_limit_bytes=VMEM_LIMIT),
    )(*args)
    return result[0] if single else result


def exchange(x):
    return lax.all_to_all(x, ("gx", "gz"), split_axis=0, concat_axis=0, tiled=True)


def gathered(x):
    copies = jnp.broadcast_to(x[None], (lax.axis_size("gz"),) + x.shape)
    out = lax.all_to_all(copies, "gz", split_axis=0, concat_axis=0, tiled=True)
    return out.reshape(-1, x.shape[1])


def neighbours(field, axis, dim, width, wrap):
    size, length = lax.axis_size(axis), field.shape[dim]
    up = [(i, (i + 1) % size) for i in range(size if wrap else size - 1)]
    down = [(j, i) for i, j in up]
    before = lax.ppermute(lax.slice_in_dim(field, length - width, length, axis=dim), axis, up)
    after = lax.ppermute(lax.slice_in_dim(field, 0, width, axis=dim), axis, down)
    return before, after


def remap(m, lower, upper, shift):
    return m + 0.5 * shift * (upper - lower) + 0.5 * shift * shift * (upper - 2.0 * m + lower)


def shards(elevation, potential, tracer, wind_speed):
    rows, length = elevation.shape
    gz = lax.axis_size("gz")
    gx = lax.axis_size("gx")
    parts = gx * gz
    depth = (length // 2) // parts
    wide = 2 * rows
    forward, inverse, odd = [jnp.asarray(t) for t in row_tables(length)]
    matrix, small = [jnp.asarray(t) for t in column_tables(length, parts)]
    device = lax.axis_index("gx") * gz + lax.axis_index("gz")
    waves = jnp.asarray(signed_wave(slot_waves(length), length).reshape(-1).astype(np.float32))
    mine = lax.dynamic_slice_in_dim(waves, device * depth, depth)
    mine = jnp.concatenate([mine, jnp.full((8,), np.float32(-np.pi))])
    wave_y = jnp.broadcast_to(mine[:, None], (depth + 8, wide))
    flag = jnp.broadcast_to((device == 0).astype(jnp.float32), (8, wide))
    half = (length // 2, wide)
    field = (rows, length)

    buffers = [pltpu.VMEM(half, jnp.float32)] * 24
    fields = [pltpu.VMEM(field, jnp.float32)] * 5
    operands = (elevation, potential, flag, wave_y, forward, inverse, odd, matrix, small)
    spec = pl.BlockSpec(memory_space=pltpu.VMEM)
    new_elevation = pl.pallas_call(
        functools.partial(surface_kernel, gx, gz),
        out_shape=jax.ShapeDtypeStruct(field, jnp.float32),
        in_specs=[spec] * len(operands),
        out_specs=spec,
        scratch_shapes=buffers
        + fields
        + [pltpu.SemaphoreType.DMA((12,)), pltpu.SemaphoreType.DMA((12,))],
        compiler_params=pltpu.CompilerParams(
            vmem_limit_bytes=VMEM_LIMIT, collective_id=0, has_side_effects=True
        ),
    )(*operands)

    air = tracer.shape[2]
    west, east = neighbours(tracer, "gx", 0, 1, True)
    eastern = jnp.concatenate([tracer[1:], east], 0)
    western = jnp.concatenate([west, tracer[:-1]], 0)
    northern = jnp.concatenate([tracer[:, :, 1:], tracer[:, :, -1:]], 2)
    southern = jnp.concatenate([tracer[:, :, :1], tracer[:, :, :-1]], 2)
    moved = tracer + DT_AIR * (
        -wind_speed * (eastern - western) * 0.5
        + NU_AIR * (eastern + western + northern + southern - 4.0 * tracer)
    )
    below, above = neighbours(moved, "gz", 1, 2, False)
    bottom = lax.axis_index("gz") == 0
    top = lax.axis_index("gz") == gz - 1
    below_near = jnp.where(bottom, moved[:, :1], below[:, 1:])
    above_near = jnp.where(top, moved[:, -1:], above[:, :1])

    window = new_elevation[:, :air]
    share = air // parts
    turned = window.reshape(rows, parts, share).transpose(1, 2, 0)
    turned = exchange(turned)
    slopes = call(slope_kernel, (parts, share, rows), turned, matrix, small)
    slopes = slopes.reshape(gx, 1, gz, share, rows)
    slopes = jnp.broadcast_to(slopes, (gx, gz, gz, share, rows)).reshape(parts, gz, share, rows)
    slopes = exchange(slopes)
    slope_rows = slopes.transpose(1, 3, 0, 2).reshape(gz * rows, air)
    old_rows = gathered(elevation[:, :air])
    new_rows = gathered(window)

    levels = tracer.shape[1]
    level_count = levels * gz
    base = lax.axis_index("gz") * levels
    level = (base - 1 + jnp.arange(levels + 2, dtype=jnp.int32)).astype(jnp.float32)
    lift = (1.0 - (level + 0.5) / level_count)[None, :, None]
    rise = ((new_rows - old_rows) / (COLUMN_DEPTH - old_rows))[:, None, :]
    shift = rise * lift[:, 1:-1] * level_count
    lower = jnp.concatenate([below_near, moved[:, :-1]], 1)
    upper = jnp.concatenate([moved[:, 1:], above_near], 1)
    remapped = remap(moved, lower, upper, shift)
    r_below = remap(below[:, 1:], below[:, :1], moved[:, :1], rise * lift[:, :1] * level_count)
    r_above = remap(above[:, :1], moved[:, -1:], above[:, 1:], rise * lift[:, -1:] * level_count)
    r_below = jnp.where(bottom, remapped[:, :1], r_below)
    r_above = jnp.where(top, remapped[:, -1:], r_above)
    lower = jnp.concatenate([r_below, remapped[:, :-1]], 1)
    upper = jnp.concatenate([remapped[:, 1:], r_above], 1)
    column = (COLUMN_DEPTH - new_rows)[:, None, :]
    advection = (
        wind_speed * lift[:, 1:-1] * slope_rows[:, None, :] / column
        * (upper - lower) * (0.5 * level_count)
    )
    spread = (
        NU_AIR * (upper - 2.0 * remapped + lower) * (level_count * level_count) / (column * column)
    )
    new_tracer = remapped + DT_AIR * (advection + spread)
    return (new_elevation, new_tracer)


def solution(mesh):
    return jax.shard_map(
        shards,
        mesh=mesh,
        in_specs=(
            P(("gx", "gz"), None),
            P(("gx", "gz"), None),
            P("gx", "gz", None),
            P("gx", "gz", None),
        ),
        out_specs=(P(("gx", "gz"), None), P("gx", "gz", None)),
        check_vma=False,
    )
```

```python
import functools

import jax
import jax.numpy as jnp
import numpy as np
import ml_dtypes
from jax import lax
from jax.experimental import pallas as pl
from jax.experimental.pallas import tpu as pltpu
from jax.sharding import PartitionSpec as P

DT_WAVE = 0.05
COLUMN_DEPTH = 32.0
DT_AIR = 0.1
NU_AIR = 0.2
INNER = 128
VMEM_LIMIT = 60 * 1024 * 1024


def split_hi_lo(matrix):
    matrix = matrix.astype(np.float32)
    hi = matrix.astype(ml_dtypes.bfloat16)
    lo = (matrix - hi.astype(np.float32)).astype(ml_dtypes.bfloat16)
    return np.stack([hi, lo])


def slot_waves(length):
    outer = length // INNER
    half = INNER // 2
    lane = np.arange(INNER)
    first = np.where(lane < half, outer * lane, outer // 2 + outer * (lane - half))
    rest = [j + outer * lane for j in range(1, outer // 2)]
    return np.stack([first] + rest)


def signed_wave(k, length):
    k = k % length
    return np.where(k < length // 2, k, k - length) * (2 * np.pi / length)


@functools.lru_cache(None)
def row_tables(length):
    outer = length // INNER
    groups = outer // 2
    half = INNER // 2
    b = np.arange(INNER)
    waves = slot_waves(length)
    forward = np.zeros((groups, 2 * INNER, 2 * INNER))
    inverse = np.zeros((groups, 2 * INNER, 2 * INNER))
    for j in range(groups):
        theta = 2 * np.pi * ((b[:, None] * waves[j][None, :]) % length) / length
        c, s = np.cos(theta), np.sin(theta)
        if j:
            forward[j] = np.block([[c, -s], [s, c]])
            inverse[j] = 2.0 * np.block([[c.T, s.T], [-s.T, c.T]]) / length
            continue
        for part, cols in ((0, slice(0, half)), (1, slice(half, INNER))):
            rows = slice(part * INNER, (part + 1) * INNER)
            imag = slice(INNER + cols.start, INNER + cols.stop)
            forward[j][rows, cols] = c[:, cols]
            forward[j][rows, imag] = -s[:, cols]
            inverse[j][cols, rows] = 2.0 * c[:, cols].T / length
            inverse[j][imag, rows] = -2.0 * s[:, cols].T / length
        alternating = np.where(b % 2 == 0, 1.0, -1.0)
        forward[j][:INNER, INNER] = alternating
        inverse[j][0, :INNER] = 1.0 / length
        inverse[j][INNER, :INNER] = alternating / length
    odd = signed_wave(waves, length)
    odd[0, 0] = 0.0
    odd = np.concatenate([-odd, odd], 1).astype(np.float32)
    return split_hi_lo(forward), split_hi_lo(inverse), odd


@functools.lru_cache(None)
def column_tables(length, parts):
    rows = length // parts
    i = np.arange(rows)
    theta = 2 * np.pi * ((i[:, None] * i[None, :]) % rows) / rows
    c, s = np.cos(theta), np.sin(theta)
    forward = np.block([[c, -s], [s, c]])
    inverse = np.block([[c, s], [-s, c]]) / length
    k1 = np.arange(parts)
    twist = 2 * np.pi * ((k1[:, None] * i[None, :]) % length) / length
    cosine = np.concatenate([np.cos(twist)] * 2, 1)
    sine = np.concatenate([np.sin(twist), -np.sin(twist)], 1)
    k = k1[:, None] + parts * i[None, :]
    wave = signed_wave(k, length)
    odd = np.where(k == length // 2, 0.0, wave)
    wave = np.concatenate([wave, wave], 1)
    odd = np.concatenate([-odd, odd], 1)
    small = np.stack([cosine, sine, wave, odd]).astype(np.float32)
    return np.stack([split_hi_lo(forward), split_hi_lo(inverse)]), small


def dot3(x, hi_matrix, lo_matrix):
    hi = x.astype(jnp.bfloat16)
    lo = (x - hi.astype(jnp.float32)).astype(jnp.bfloat16)
    out = jnp.dot(hi, hi_matrix, preferred_element_type=jnp.float32)
    out += jnp.dot(lo, hi_matrix, preferred_element_type=jnp.float32)
    return out + jnp.dot(hi, lo_matrix, preferred_element_type=jnp.float32)


def constant_product(value, factor):
    if abs(factor) < 1e-12:
        return None
    if abs(factor - 1) < 1e-12:
        return value
    if abs(factor + 1) < 1e-12:
        return -value
    return value * np.float32(factor)


def total(terms):
    terms = [t for t in terms if t is not None]
    result = terms[0]
    for t in terms[1:]:
        result = result + t
    return result


def row_forward(field, table):
    outer = field.shape[1] // INNER
    half = outer // 2
    x = [field[:, a * INNER : (a + 1) * INNER] for a in range(outer)]
    plus = [x[a] + x[outer - a] for a in range(1, half)]
    minus = [x[a] - x[outer - a] for a in range(1, half)]
    ends = [x[0] + x[half], x[0] - x[half]]
    quarter = half // 2

    def real_of(k):
        sign = 1 if k % 2 == 0 else -1
        folded = []
        for a in range(1, quarter):
            both = plus[a - 1] + plus[half - a - 1] if sign > 0 else plus[a - 1] - plus[half - a - 1]
            folded.append(constant_product(both, np.cos(2 * np.pi * a * k / outer)))
        folded.append(constant_product(plus[quarter - 1], np.cos(2 * np.pi * quarter * k / outer)))
        return total([ends[k % 2]] + folded)

    def imag_of(k):
        folded = []
        for a in range(1, quarter):
            both = minus[a - 1] - minus[half - a - 1] if k % 2 == 0 else minus[a - 1] + minus[half - a - 1]
            folded.append(constant_product(both, -np.sin(2 * np.pi * a * k / outer)))
        folded.append(constant_product(minus[quarter - 1], -np.sin(2 * np.pi * quarter * k / outer)))
        return total(folded)

    groups = []
    for j in range(half):
        if j == 0:
            pair = jnp.concatenate([real_of(0), real_of(half)], 1)
        else:
            pair = jnp.concatenate([real_of(j), imag_of(j)], 1)
        groups.append(dot3(pair, table[0, j], table[1, j]))
    return groups


def row_inverse(groups, table):
    half = len(groups)
    outer = 2 * half
    y = [dot3(groups[j], table[0, j], table[1, j]) for j in range(half)]
    re = [v[:, :INNER] for v in y]
    im = [v[:, INNER:] for v in y]
    ends = [re[0] + im[0], re[0] - im[0]]
    blocks = [None] * outer
    for a in range(half + 1):
        even = total(
            [ends[a % 2]]
            + [constant_product(re[k], np.cos(2 * np.pi * a * k / outer)) for k in range(1, half)]
        )
        if a % half == 0:
            blocks[a] = even
            continue
        odd = total([constant_product(im[k], np.sin(2 * np.pi * a * k / outer)) for k in range(1, half)])
        blocks[a] = even - odd
        blocks[outer - a] = even + odd
    return jnp.concatenate(blocks, 1)


def put_groups(groups, out_ref):
    for j, g in enumerate(groups):
        both = jnp.concatenate([g[:, :INNER], g[:, INNER:]], 0)
        out_ref[j * INNER : (j + 1) * INNER, :] = both.T


def get_groups(in_ref):
    groups = []
    for j in range(in_ref.shape[0] // INNER):
        both = in_ref[j * INNER : (j + 1) * INNER, :].T
        rows = both.shape[0] // 2
        groups.append(jnp.concatenate([both[:rows], both[rows:]], 1))
    return groups


def y_derivative(groups, odd_ref, table):
    turned = []
    for j, g in enumerate(groups):
        turned.append(jnp.concatenate([g[:, INNER:], g[:, :INNER]], 1) * odd_ref[j : j + 1, :])
    return row_inverse(turned, table)


def turn(z):
    rows = z.shape[-1] // 2
    if z.shape[-1] == INNER:
        return pltpu.roll(z, rows, z.ndim - 1)
    return jnp.concatenate([z[..., rows:], z[..., :rows]], -1)


def list_transform(z, sign, signs):
    n = len(z)
    if n == 1:
        return z
    even = list_transform(z[0::2], sign, signs)
    odd = list_transform(z[1::2], sign, signs)
    first, second = [], []
    for k in range(n // 2):
        t = odd[k]
        if k:
            angle = sign * 2 * np.pi * k / n
            t = total(
                [
                    constant_product(t, np.cos(angle)),
                    turn(t) * (signs * np.float32(np.sin(angle))),
                ]
            )
        first.append(even[k] + t)
        second.append(even[k] - t)
    return first + second


def lane_signs(shape):
    lane = lax.broadcasted_iota(jnp.int32, shape, 1)
    return jnp.where(lane < shape[1] // 2, -1.0, 1.0).astype(jnp.float32)


def column_forward(z, matrix, small):
    y = list_transform(z, -1, lane_signs(z[0].shape))
    depth = z[0].shape[0]
    y = [v * small[0, k : k + 1] + turn(v) * small[1, k : k + 1] for k, v in enumerate(y)]
    out = dot3(jnp.concatenate(y, 0), matrix[0, 0], matrix[0, 1])
    return [out[k * depth : (k + 1) * depth] for k in range(len(z))]


def column_inverse(spectrum, matrix, small):
    depth = spectrum[0].shape[0]
    out = dot3(jnp.concatenate(spectrum, 0), matrix[1, 0], matrix[1, 1])
    y = [out[k * depth : (k + 1) * depth] for k in range(len(spectrum))]
    y = [v * small[0, k : k + 1] - turn(v) * small[1, k : k + 1] for k, v in enumerate(y)]
    return list_transform(y, 1, lane_signs(y[0].shape))


def open_columns(in_ref, parts, first_mask, second_mask):
    z = []
    depth = in_ref.shape[0] // parts
    for s in range(parts):
        head = in_ref[s * depth : s * depth + 8]
        extra = turn(head) * first_mask
        head = head * (1.0 - second_mask)
        body = [in_ref[s * depth + 8 : (s + 1) * depth]] if depth > 8 else []
        z.append(jnp.concatenate([head] + body + [extra], 0))
    return z


def close_columns(z, out_ref, second_mask):
    for s, block in enumerate(z):
        depth = block.shape[0] - 8
        head = block[:8] * (1.0 - second_mask) + turn(block[depth:]) * second_mask
        out_ref[s * depth : s * depth + 8] = head
        if depth > 8:
            out_ref[s * depth + 8 : (s + 1) * depth] = block[8:depth]


def masks(flag_ref):
    flag = flag_ref[...]
    row = lax.broadcasted_iota(jnp.int32, flag.shape, 0)
    lane = lax.broadcasted_iota(jnp.int32, flag.shape, 1)
    left = lane < flag.shape[1] // 2
    return (
        jnp.where((row == 0) & left, flag, 0.0),
        jnp.where((row == 0) & jnp.logical_not(left), flag, 0.0),
    )


def slope_kernel(in_ref, matrix, small, out_ref):
    rows = in_ref.shape[2]
    z = []
    for s in range(in_ref.shape[0]):
        block = in_ref[s]
        z.append(jnp.concatenate([block, jnp.zeros_like(block)], 1))
    spectrum = column_forward(z, matrix, small)
    work = [turn(v) * small[3, k : k + 1] for k, v in enumerate(spectrum)]
    for s, block in enumerate(column_inverse(work, matrix, small)):
        out_ref[s] = block[:, :rows]


def surface_kernel(
    gx, gz, e_ref, p_ref, flag_ref, wave_ref, forward, inverse, odd, matrix, small,
    out_ref, *scratch,
):
    parts = gx * gz
    count = 12
    sent = scratch[:count]
    came = scratch[count : 2 * count]
    slope_y_ref, speed_y_ref, first_ref, twice_ref, part_ref, send_sem, recv_sem = scratch[2 * count :]
    depth = sent[0].shape[0] // parts
    at_x, at_z = lax.axis_index("gx"), lax.axis_index("gz")
    me = at_x * gz + at_z
    barrier = pltpu.get_barrier_semaphore()

    def peer_of(step):
        peer = lax.rem(me + step, parts)
        return peer, (peer // gz, lax.rem(peer, gz))

    def greet(step, carry):
        _, place = peer_of(step)
        pl.semaphore_signal(barrier, inc=1, device_id=place, device_id_type=pl.DeviceIdType.MESH)
        return carry

    def rows_at(index):
        return pl.ds(pl.multiple_of(index * depth, depth), depth)

    def send(k):
        def body(step, carry):
            peer, place = peer_of(step)
            pltpu.make_async_remote_copy(
                src_ref=sent[k].at[rows_at(peer)],
                dst_ref=came[k].at[rows_at(me)],
                send_sem=send_sem.at[k],
                recv_sem=recv_sem.at[k],
                device_id=place,
                device_id_type=pl.DeviceIdType.MESH,
            ).start()
            return carry

        lax.fori_loop(1, parts, body, 0)
        came[k][rows_at(me), :] = sent[k][rows_at(me), :]

    def whole(k):
        most = pl.ds(0, (parts - 1) * depth)
        return pltpu.make_async_remote_copy(
            src_ref=sent[k].at[most],
            dst_ref=came[k].at[most],
            send_sem=send_sem.at[k],
            recv_sem=recv_sem.at[k],
            device_id=peer_of(1)[1],
            device_id_type=pl.DeviceIdType.MESH,
        )

    def fetch(k):
        whole(k).wait_recv()

    first_mask, second_mask = masks(flag_ref)
    wave_y = wave_ref[...]
    y_squared = wave_y * wave_y

    def spectrum_of(k):
        return column_forward(open_columns(came[k], parts, first_mask, second_mask), matrix, small)

    def raised(spectrum, power, k):
        work = []
        for j, v in enumerate(spectrum):
            square = small[2, j : j + 1] * small[2, j : j + 1] + y_squared
            if power == 1:
                factor = jnp.sqrt(square)
            elif power == 2:
                factor = square
            else:
                factor = square * jnp.sqrt(square)
            work.append(v * factor)
        close_columns(column_inverse(work, matrix, small), sent[k], second_mask)

    def along_x(spectrum, k):
        work = [turn(v) * small[3, j : j + 1] for j, v in enumerate(spectrum)]
        close_columns(column_inverse(work, matrix, small), sent[k], second_mask)

    def field_of(k):
        return row_inverse(get_groups(came[k]), inverse)

    P0, E0, A0, A1, A2, VX, SX, S0, B0, B1, T0, C0 = range(count)
    lax.fori_loop(1, parts, greet, 0)
    p_groups = row_forward(p_ref[...], forward)
    put_groups(p_groups, sent[P0])
    pl.semaphore_wait(barrier, parts - 1)
    send(P0)
    e_groups = row_forward(e_ref[...], forward)
    put_groups(e_groups, sent[E0])
    send(E0)
    slope_y_ref[...] = y_derivative(e_groups, odd, inverse)
    speed_y_ref[...] = y_derivative(p_groups, odd, inverse)

    fetch(P0)
    p_spectrum = spectrum_of(P0)
    raised(p_spectrum, 1, A0)
    send(A0)
    raised(p_spectrum, 2, A1)
    send(A1)
    raised(p_spectrum, 3, A2)
    along_x(p_spectrum, VX)
    fetch(E0)
    along_x(spectrum_of(E0), SX)

    fetch(A0)
    first_ref[...] = field_of(A0)
    put_groups(row_forward(-e_ref[...] * first_ref[...], forward), sent[S0])
    send(S0)
    send(A2)
    fetch(A1)
    twice_ref[...] = field_of(A1)
    elevation = e_ref[...]
    part_ref[...] = first_ref[...] + elevation * twice_ref[...]

    fetch(S0)
    s_spectrum = spectrum_of(S0)
    raised(s_spectrum, 1, B0)
    send(B0)
    send(VX)
    raised(s_spectrum, 2, B1)
    fetch(A2)
    elevation = e_ref[...]
    part_ref[...] += 0.5 * elevation * elevation * field_of(A2)

    fetch(B0)
    once = field_of(B0)
    elevation = e_ref[...]
    third = -elevation * once - 0.5 * elevation * elevation * twice_ref[...]
    put_groups(row_forward(third, forward), sent[T0])
    send(T0)
    send(SX)
    send(B1)
    part_ref[...] += once
    fetch(VX)
    first_ref[...] = field_of(VX)

    fetch(T0)
    raised(spectrum_of(T0), 1, C0)
    send(C0)
    fetch(SX)
    slope_x = field_of(SX)
    slope_y = slope_y_ref[...]
    twice_ref[...] = 1.0 + slope_x * slope_x + slope_y * slope_y
    first_ref[...] = slope_x * first_ref[...] + slope_y * speed_y_ref[...]
    fetch(B1)
    part_ref[...] += e_ref[...] * field_of(B1)
    fetch(C0)
    vertical = part_ref[...] + field_of(C0)
    out_ref[...] = e_ref[...] + DT_WAVE * (twice_ref[...] * vertical - first_ref[...])
    for k in range(count):
        whole(k).wait_send()


def call(kernel, out_shapes, *args):
    single = not isinstance(out_shapes, list)
    shapes = [out_shapes] if single else out_shapes
    spec = pl.BlockSpec(memory_space=pltpu.VMEM)
    result = pl.pallas_call(
        kernel,
        out_shape=[jax.ShapeDtypeStruct(s, jnp.float32) for s in shapes],
        in_specs=[spec] * len(args),
        out_specs=[spec] * len(shapes),
        compiler_params=pltpu.CompilerParams(vmem_limit_bytes=VMEM_LIMIT),
    )(*args)
    return result[0] if single else result


def exchange(x):
    return lax.all_to_all(x, ("gx", "gz"), split_axis=0, concat_axis=0, tiled=True)


def gathered(x):
    copies = jnp.broadcast_to(x[None], (lax.axis_size("gz"),) + x.shape)
    out = lax.all_to_all(copies, "gz", split_axis=0, concat_axis=0, tiled=True)
    return out.reshape(-1, x.shape[1])


def neighbours(field, axis, dim, width, wrap):
    size, length = lax.axis_size(axis), field.shape[dim]
    up = [(i, (i + 1) % size) for i in range(size if wrap else size - 1)]
    down = [(j, i) for i, j in up]
    before = lax.ppermute(lax.slice_in_dim(field, length - width, length, axis=dim), axis, up)
    after = lax.ppermute(lax.slice_in_dim(field, 0, width, axis=dim), axis, down)
    return before, after


def remap(m, lower, upper, shift):
    return m + 0.5 * shift * (upper - lower) + 0.5 * shift * shift * (upper - 2.0 * m + lower)


def shards(elevation, potential, tracer, wind_speed):
    rows, length = elevation.shape
    gz = lax.axis_size("gz")
    gx = lax.axis_size("gx")
    parts = gx * gz
    depth = (length // 2) // parts
    wide = 2 * rows
    forward, inverse, odd = [jnp.asarray(t) for t in row_tables(length)]
    matrix, small = [jnp.asarray(t) for t in column_tables(length, parts)]
    device = lax.axis_index("gx") * gz + lax.axis_index("gz")
    waves = jnp.asarray(signed_wave(slot_waves(length), length).reshape(-1).astype(np.float32))
    mine = lax.dynamic_slice_in_dim(waves, device * depth, depth)
    mine = jnp.concatenate([mine, jnp.full((8,), np.float32(-np.pi))])
    wave_y = jnp.broadcast_to(mine[:, None], (depth + 8, wide))
    flag = jnp.broadcast_to((device == 0).astype(jnp.float32), (8, wide))
    half = (length // 2, wide)
    field = (rows, length)

    buffers = [pltpu.VMEM(half, jnp.float32)] * 24
    fields = [pltpu.VMEM(field, jnp.float32)] * 5
    operands = (elevation, potential, flag, wave_y, forward, inverse, odd, matrix, small)
    spec = pl.BlockSpec(memory_space=pltpu.VMEM)
    new_elevation = pl.pallas_call(
        functools.partial(surface_kernel, gx, gz),
        out_shape=jax.ShapeDtypeStruct(field, jnp.float32),
        in_specs=[spec] * len(operands),
        out_specs=spec,
        scratch_shapes=buffers
        + fields
        + [pltpu.SemaphoreType.DMA((12,)), pltpu.SemaphoreType.DMA((12,))],
        compiler_params=pltpu.CompilerParams(
            vmem_limit_bytes=VMEM_LIMIT, collective_id=0, has_side_effects=True
        ),
    )(*operands)

    air = tracer.shape[2]
    west, east = neighbours(tracer, "gx", 0, 1, True)
    eastern = jnp.concatenate([tracer[1:], east], 0)
    western = jnp.concatenate([west, tracer[:-1]], 0)
    northern = jnp.concatenate([tracer[:, :, 1:], tracer[:, :, -1:]], 2)
    southern = jnp.concatenate([tracer[:, :, :1], tracer[:, :, :-1]], 2)
    moved = tracer + DT_AIR * (
        -wind_speed * (eastern - western) * 0.5
        + NU_AIR * (eastern + western + northern + southern - 4.0 * tracer)
    )
    below, above = neighbours(moved, "gz", 1, 2, False)
    bottom = lax.axis_index("gz") == 0
    top = lax.axis_index("gz") == gz - 1
    below_near = jnp.where(bottom, moved[:, :1], below[:, 1:])
    above_near = jnp.where(top, moved[:, -1:], above[:, :1])

    window = new_elevation[:, :air]
    share = air // parts
    turned = window.reshape(rows, parts, share).transpose(1, 2, 0)
    turned = exchange(turned)
    slopes = call(slope_kernel, (parts, share, rows), turned, matrix, small)
    slopes = slopes.reshape(gx, 1, gz, share, rows)
    slopes = jnp.broadcast_to(slopes, (gx, gz, gz, share, rows)).reshape(parts, gz, share, rows)
    slopes = exchange(slopes)
    slope_rows = slopes.transpose(1, 3, 0, 2).reshape(gz * rows, air)
    both = gathered(jnp.concatenate([elevation[:, :air], window], 1))
    old_rows, new_rows = both[:, :air], both[:, air:]

    levels = tracer.shape[1]
    level_count = levels * gz
    base = lax.axis_index("gz") * levels
    level = (base - 1 + jnp.arange(levels + 2, dtype=jnp.int32)).astype(jnp.float32)
    lift = (1.0 - (level + 0.5) / level_count)[None, :, None]
    rise = ((new_rows - old_rows) / (COLUMN_DEPTH - old_rows))[:, None, :]
    shift = rise * lift[:, 1:-1] * level_count
    lower = jnp.concatenate([below_near, moved[:, :-1]], 1)
    upper = jnp.concatenate([moved[:, 1:], above_near], 1)
    remapped = remap(moved, lower, upper, shift)
    r_below = remap(below[:, 1:], below[:, :1], moved[:, :1], rise * lift[:, :1] * level_count)
    r_above = remap(above[:, :1], moved[:, -1:], above[:, 1:], rise * lift[:, -1:] * level_count)
    r_below = jnp.where(bottom, remapped[:, :1], r_below)
    r_above = jnp.where(top, remapped[:, -1:], r_above)
    lower = jnp.concatenate([r_below, remapped[:, :-1]], 1)
    upper = jnp.concatenate([remapped[:, 1:], r_above], 1)
    column = (COLUMN_DEPTH - new_rows)[:, None, :]
    advection = (
        wind_speed * lift[:, 1:-1] * slope_rows[:, None, :] / column
        * (upper - lower) * (0.5 * level_count)
    )
    spread = (
        NU_AIR * (upper - 2.0 * remapped + lower) * (level_count * level_count) / (column * column)
    )
    new_tracer = remapped + DT_AIR * (advection + spread)
    return (new_elevation, new_tracer)


def solution(mesh):
    return jax.shard_map(
        shards,
        mesh=mesh,
        in_specs=(
            P(("gx", "gz"), None),
            P(("gx", "gz"), None),
            P("gx", "gz", None),
            P("gx", "gz", None),
        ),
        out_specs=(P(("gx", "gz"), None), P("gx", "gz", None)),
        check_vma=False,
    )
```
